32 devices in a mesh: replica: 4 (over z), fsdp: 4 (over y, x), ctx: 2 (over core).
Axes of the slice: x: 2, y: 2, z: 4, core: 2. Of those that a mesh axis runs over, the one named last changes fastest.
Arguments:
- tokens: bfloat16 [32, 1024, 1024], P(('replica', 'fsdp'), 'ctx'), may hold values from -6 to 6
- segments: int32 [32, 1024], P(('replica', 'fsdp')), may hold values from 0 to 2, as said below
- attn_gain: bfloat16 [1024], P(('fsdp', 'ctx')), may hold values from 0.25 to 1.75
- query_weight: bfloat16 [1024, 1024], P(('fsdp', 'ctx')), may hold values from -0.1875 to 0.1875
- key_weight: bfloat16 [1024, 512], P(('fsdp', 'ctx')), may hold values from -0.1875 to 0.1875
- value_weight: bfloat16 [1024, 512], P(('fsdp', 'ctx')), may hold values from -0.1875 to 0.1875
- output_weight: bfloat16 [1024, 1024], P(('fsdp', 'ctx')), may hold values from -0.75 to 0.75
- query_gain: bfloat16 [64], P(('fsdp', 'ctx')), may hold values from 0.25 to 1.75
- key_gain: bfloat16 [64], P(('fsdp', 'ctx')), may hold values from 0.25 to 1.75
- ffn_gain: bfloat16 [1024], P(('fsdp', 'ctx')), may hold values from 0.25 to 1.75
- gate_weight: bfloat16 [1024, 4608], P(('fsdp', 'ctx')), may hold values from -0.1875 to 0.1875
- up_weight: bfloat16 [1024, 4608], P(('fsdp', 'ctx')), may hold values from -0.1875 to 0.1875
- down_weight: bfloat16 [4608, 1024], P(('fsdp', 'ctx')), may hold values from -0.09375 to 0.09375
- cotangent: bfloat16 [32, 1024, 1024], P(('replica', 'fsdp'), 'ctx'), may hold values from -6 to 6
Outputs:
- output: bfloat16 [32, 1024, 1024], P(('replica', 'fsdp'), 'ctx')
- input_grad: float32 [32, 1024, 1024], P(('replica', 'fsdp'), 'ctx')
- grad_attn_gain: float32 [1024], P(('fsdp', 'ctx'))
- grad_w_query: float32 [1024, 1024], P(('fsdp', 'ctx'))
- grad_w_key: float32 [1024, 512], P(('fsdp', 'ctx'))
- grad_w_value: float32 [1024, 512], P(('fsdp', 'ctx'))
- grad_w_out: float32 [1024, 1024], P(('fsdp', 'ctx'))
- grad_query_gain: float32 [64], P(('fsdp', 'ctx'))
- grad_key_gain: float32 [64], P(('fsdp', 'ctx'))
- grad_ffn_gain: float32 [1024], P(('fsdp', 'ctx'))
- grad_w_gate: float32 [1024, 4608], P(('fsdp', 'ctx'))
- grad_w_up: float32 [1024, 4608], P(('fsdp', 'ctx'))
- grad_w_down: float32 [4608, 1024], P(('fsdp', 'ctx'))
The draws below stay inside these ranges and needn't reach their ends.
Inputs may be any that keep to these rules, and one draw needn't show every extreme that they name: `segments`: never falls along a sequence; every sequence holds documents 0, 1 and 2, each of one token or more, and document 1 holds positions 256 to 767.
All inputs are finite; a program needn't handle non-finite values.
Results may differ from the reference program's by a relative error of at most 0.028.
Values may be sent and summed in bfloat16 or wider, within the bound.
A program may use at most 256 MiB of HBM per device.

```python
import math
import jax
import jax.numpy as jnp
from jax import lax

D = 1024
HEADS = 16
KV_HEADS = 8
HEAD_DIM = 64
FF = 4608
SEQLEN = 1024
SEQS = 32


def draw_segments(key, part):
    key = jax.random.fold_in(key, 17)
    first_key, second_key = jax.random.split(key)
    first_cut = jax.random.randint(first_key, (SEQS, 1), 1, SEQLEN // 4 + 1)
    second_cut = jax.random.randint(second_key, (SEQS, 1), 3 * SEQLEN // 4, SEQLEN)
    places = jnp.arange(SEQLEN, dtype=jnp.int32)[None, :]
    return (places >= first_cut).astype(jnp.int32) + (places >= second_cut).astype(jnp.int32)


def shard_levels(own_key, extent, pieces, least, largest):
    def one(axis_at, blocks):
        draws = jax.random.uniform(jax.random.fold_in(jax.random.fold_in(own_key, 6), axis_at), (blocks,), jnp.float32, least / len(pieces), largest / len(pieces))
        return jnp.repeat(jnp.exp(draws), extent[axis_at] // blocks).reshape((-1,) + (1,) * (len(extent) - axis_at - 1))

    factor_of = one(*pieces[0])
    for cut in pieces[1:]:
        factor_of = factor_of * one(*cut)
    return factor_of


def scatter_about(rng, shape, deviation, reach, cuts=(), kind=jnp.bfloat16):
    entries = jax.random.normal(rng, shape, jnp.float32) * deviation
    if len(cuts) > 0:
        entries = shard_levels(rng, shape, cuts, -0.22, 0.18) * entries
    return jnp.clip(entries, min=-reach, max=reach).astype(kind)


def setup_inputs(seed: int = 0) -> dict:
    streams_of = jax.random.split(jax.random.key(seed), 15)
    tokens = scatter_about(streams_of[0], (SEQS, SEQLEN, D), 1.0, 6.0, ((0, 16), (1, 2)))
    segments = draw_segments(jax.random.fold_in(streams_of[14], 71), 0)
    attn_gain = jnp.clip(1.0 + 0.15 * jax.random.normal(streams_of[2], (D,), jnp.float32), 0.25, 1.75).astype(jnp.bfloat16)
    query_weight = scatter_about(streams_of[3], (D, HEADS * HEAD_DIM), D ** -0.5, 0.1875, ((0, 8),))
    key_weight = scatter_about(streams_of[4], (D, KV_HEADS * HEAD_DIM), D ** -0.5, 0.1875, ((0, 8),))
    value_weight = scatter_about(streams_of[5], (D, KV_HEADS * HEAD_DIM), D ** -0.5, 0.1875, ((0, 8),))
    output_weight = scatter_about(streams_of[6], (HEADS * HEAD_DIM, D), (HEADS * HEAD_DIM // 16) ** -0.5, 0.75, ((0, 8),))
    query_gain = jnp.clip(1.0 + 0.15 * jax.random.normal(streams_of[7], (HEAD_DIM,), jnp.float32), 0.25, 1.75).astype(jnp.bfloat16)
    key_gain = jnp.clip(1.0 + 0.15 * jax.random.normal(streams_of[8], (HEAD_DIM,), jnp.float32), 0.25, 1.75).astype(jnp.bfloat16)
    ffn_gain = jnp.clip(1.0 + 0.15 * jax.random.normal(streams_of[9], (D,), jnp.float32), 0.25, 1.75).astype(jnp.bfloat16)
    gate_weight = scatter_about(streams_of[10], (D, FF), D ** -0.5, 0.1875, ((0, 8),))
    up_weight = scatter_about(streams_of[11], (D, FF), D ** -0.5, 0.1875, ((0, 8),))
    down_weight = scatter_about(streams_of[12], (FF, D), FF ** -0.5, 0.09375, ((0, 8),))
    cotangent = scatter_about(streams_of[13], (SEQS, SEQLEN, D), 1.0, 6.0, ((0, 16), (1, 2)))
    return {"tokens": tokens, "segments": segments, "attn_gain": attn_gain, "query_weight": query_weight, "key_weight": key_weight, "value_weight": value_weight, "output_weight": output_weight, "query_gain": query_gain, "key_gain": key_gain, "ffn_gain": ffn_gain, "gate_weight": gate_weight, "up_weight": up_weight, "down_weight": down_weight, "cotangent": cotangent}


epsilon = 1e-05
rope_base = 1000000.0
neg_fill = -1e+30
full_precision = lax.Precision.HIGHEST

@jax.custom_vjp
def reduced_precision(v):
    return lax.optimization_barrier(v.astype(jnp.bfloat16)).astype(jnp.float32)

@jax.custom_vjp
def reduced_backward(v):
    return v

def low_keep(v):
    return (reduced_precision(v), None)

def low_pass(kept, grad):
    return (grad,)

def back_keep(v):
    return (v, None)

def back_low(kept, grad):
    return (reduced_precision(grad),)
reduced_precision.defvjp(low_keep, low_pass)
reduced_backward.defvjp(back_keep, back_low)

def rms_scale(values):
    return lax.rsqrt(lax.optimization_barrier(jnp.mean(values * values, axis=-1, keepdims=True)) + epsilon)

def rotate(values, cosine, sine):
    half_dim = values.shape[-1] // 2
    turned = jnp.concatenate([-values[..., half_dim:], values[..., :half_dim]], axis=-1)
    return values * cosine + turned * sine

def group_forward(params, input_rows, seg_block):
    gain_one, query_weight, key_weight, value_weight, output_weight, query_gain, key_gain, gain_two, gate_weight, up_weight, down_weight = params
    seq_count, seq_len = seg_block.shape
    index = jnp.arange(seq_len, dtype=jnp.int32)
    same_doc = seg_block[:, :, None] == seg_block[:, None, :]
    positions = lax.optimization_barrier(jnp.sum((same_doc & (index[None, None, :] < index[None, :, None])).astype(jnp.int32), axis=-1))
    allowed = same_doc & (index[None, None, :] <= index[None, :, None])
    freq = jnp.power(jnp.float32(rope_base), -jnp.arange(HEAD_DIM // 2, dtype=jnp.float32) * 2.0 / HEAD_DIM)
    angle = positions.astype(jnp.float32)[..., None] * freq
    angle = jnp.concatenate([angle, angle], axis=-1)[:, :, None, :]
    cosine = jnp.cos(angle)
    sine = jnp.sin(angle)
    hidden_input = reduced_precision(input_rows * rms_scale(input_rows) * gain_one)
    query_unrotated = reduced_backward(jnp.einsum('tjh,hi->tji', hidden_input, query_weight, precision=full_precision))
    key_unrotated = reduced_backward(jnp.einsum('tjh,hi->tji', hidden_input, key_weight, precision=full_precision))
    value_rows = reduced_precision(reduced_backward(jnp.einsum('tjh,hi->tji', hidden_input, value_weight, precision=full_precision)))
    query_heads = query_unrotated.reshape(seq_count, seq_len, HEADS, HEAD_DIM)
    key_heads = key_unrotated.reshape(seq_count, seq_len, KV_HEADS, HEAD_DIM)
    query = reduced_precision(reduced_backward(rotate(query_heads * rms_scale(query_heads) * query_gain, cosine, sine)))
    key = reduced_precision(reduced_backward(rotate(key_heads * rms_scale(key_heads) * key_gain, cosine, sine)))
    value_heads = value_rows.reshape(seq_count, seq_len, KV_HEADS, HEAD_DIM)
    group_size = HEADS // KV_HEADS
    query_group = query.reshape(seq_count, seq_len, KV_HEADS, group_size, HEAD_DIM)
    scores = reduced_backward(jnp.einsum('sqagd,skad->sagqk', query_group, key, precision=full_precision) * HEAD_DIM ** (-0.5))
    masked = jnp.where(allowed[:, None, None], scores, neg_fill)
    probs = reduced_precision(jax.nn.softmax(masked, axis=-1))
    attention_output = jnp.einsum('sagqk,skad->sqagd', probs, value_heads, precision=full_precision)
    attention_output = reduced_precision(reduced_backward(attention_output.reshape(seq_count, seq_len, HEADS * HEAD_DIM)))
    residual_stream = input_rows + reduced_backward(jnp.einsum('ivx,xa->iva', attention_output, output_weight, precision=full_precision))
    hidden_second = reduced_precision(residual_stream * rms_scale(residual_stream) * gain_two)
    gate_rows = reduced_backward(jnp.einsum('pui,ij->puj', hidden_second, gate_weight, precision=full_precision))
    up_projected = reduced_backward(jnp.einsum('pui,ij->puj', hidden_second, up_weight, precision=full_precision))
    activation_rows = reduced_precision(jax.nn.silu(gate_rows) * up_projected)
    return residual_stream + reduced_backward(jnp.einsum('pub,ba->pua', activation_rows, down_weight, precision=full_precision))

def reference(tokens, segments, attn_gain, query_weight, key_weight, value_weight, output_weight, query_gain, key_gain, ffn_gain, gate_weight, up_weight, down_weight, cotangent):
    input_rows = tokens.astype(jnp.float32)
    params = (attn_gain.astype(jnp.float32), query_weight.astype(jnp.float32), key_weight.astype(jnp.float32), value_weight.astype(jnp.float32), output_weight.astype(jnp.float32), query_gain.astype(jnp.float32), key_gain.astype(jnp.float32), ffn_gain.astype(jnp.float32), gate_weight.astype(jnp.float32), up_weight.astype(jnp.float32), down_weight.astype(jnp.float32))
    seq_total, seq_len, width = input_rows.shape
    block_size = math.gcd(seq_total, 4)
    block_count = seq_total // block_size
    seg_blocks = segments.reshape(block_count, block_size, seq_len)
    checked = jax.checkpoint(group_forward)

    def forward(values, weights):

        def stepper(carry, bundle):
            return (carry, checked(weights, bundle[0], bundle[1]))
        _, result = lax.scan(stepper, jnp.float32(0.0), (values.reshape(block_count, block_size, seq_len, width), seg_blocks))
        return result.reshape(seq_total, seq_len, width)
    result, pullback = jax.vjp(forward, input_rows, params)
    grad_inputs, grads = pullback(cotangent.astype(jnp.float32))
    return (result.astype(jnp.bfloat16), grad_inputs, grads[0], grads[1], grads[2], grads[3], grads[4], grads[5], grads[6], grads[7], grads[8], grads[9], grads[10])
```

```python
import jax
import jax.numpy as jnp
from jax import lax
from jax.experimental import pallas as pl
from jax.experimental.pallas import tpu as pltpu
from jax.sharding import PartitionSpec as P

epsilon = 1e-05
rope_base = 1000000.0
log2_e = 1.4426950408889634
row_block = 256
f32 = jnp.float32
bf16 = jnp.bfloat16


def rms_scale(values):
    return lax.rsqrt(jnp.mean(values * values, axis=-1, keepdims=True) + epsilon)


def norm_back(grad_in, normed, factor):
    return factor * (grad_in - normed * jnp.mean(grad_in * normed, axis=-1, keepdims=True))


def dot_nt(left, right):
    return lax.dot_general(left, right, (((1,), (1,)), ((), ())), preferred_element_type=f32)


def dot_tn(left, right):
    return lax.dot_general(left, right, (((0,), (0,)), ((), ())), preferred_element_type=f32)


def dot_nn(left, right):
    return jnp.dot(left, right, preferred_element_type=f32)


def block_mask(seg_col, seg_row, first, count):
    same = seg_col == seg_row
    row_at = first + lax.broadcasted_iota(jnp.int32, same.shape, 0)
    key_at = lax.broadcasted_iota(jnp.int32, same.shape, 1)
    return same & (key_at <= row_at)


def attend_kernel(head_dim, group, kv_per, query, key, value, seg_col, seg_row, mixed, logs):
    seq_len = query.shape[0]
    size = min(row_block, seq_len)
    factor = log2_e * head_dim**-0.5
    for first in range(0, seq_len, size):
        last = first + size
        mask = block_mask(
            seg_col[0, first:last, :], seg_row[0, :, :last], first, size
        )
        pieces = []
        log_cols = []
        for kv in range(kv_per):
            key_blk = key[:last, kv * head_dim : (kv + 1) * head_dim]
            value_blk = value[:last, kv * head_dim : (kv + 1) * head_dim]
            for member in range(group):
                at = (kv * group + member) * head_dim
                scores = dot_nt(query[first:last, at : at + head_dim], key_blk)
                expo = jnp.where(mask, jnp.exp2(scores * factor), 0.0)
                total = jnp.sum(expo, axis=-1, keepdims=True)
                out = dot_nn(expo.astype(bf16), value_blk)
                pieces.append((out / total).astype(bf16))
                log_cols.append(jnp.log2(total))
        mixed[first:last, :] = jnp.concatenate(pieces, axis=1)
        logs[0, first:last, :] = jnp.concatenate(log_cols, axis=1)


def attend_back_kernel(
    head_dim,
    group,
    kv_per,
    query,
    key,
    value,
    seg_col,
    seg_row,
    mixed,
    grad_mixed,
    logs,
    grad_query,
    grad_key,
    grad_value,
    key_sum,
    value_sum,
):
    seq_len = query.shape[0]
    size = min(row_block, seq_len)
    scale = head_dim**-0.5
    factor = log2_e * scale
    key_sum[...] = jnp.zeros_like(key_sum)
    value_sum[...] = jnp.zeros_like(value_sum)
    for first in range(0, seq_len, size):
        last = first + size
        mask = block_mask(
            seg_col[0, first:last, :], seg_row[0, :, :last], first, size
        )
        pieces = []
        for kv in range(kv_per):
            key_blk = key[:last, kv * head_dim : (kv + 1) * head_dim]
            value_blk = value[:last, kv * head_dim : (kv + 1) * head_dim]
            for member in range(group):
                head = kv * group + member
                at = head * head_dim
                query_blk = query[first:last, at : at + head_dim]
                grad_blk = grad_mixed[first:last, at : at + head_dim]
                mixed_blk = mixed[first:last, at : at + head_dim]
                delta = jnp.sum(
                    grad_blk.astype(f32) * mixed_blk.astype(f32), axis=-1, keepdims=True
                )
                scores = dot_nt(query_blk, key_blk)
                log_col = logs[0, first:last, head : head + 1]
                probs = jnp.where(mask, jnp.exp2(scores * factor - log_col), 0.0)
                grad_probs = dot_nt(grad_blk, value_blk)
                grad_scores = (probs * (grad_probs - delta)).astype(bf16)
                value_sum[kv, :last, :] += dot_tn(probs.astype(bf16), grad_blk)
                key_sum[kv, :last, :] += dot_tn(grad_scores, query_blk)
                pieces.append((dot_nn(grad_scores, key_blk) * scale).astype(bf16))
        grad_query[first:last, :] = jnp.concatenate(pieces, axis=1)
    grad_key[...] = jnp.concatenate(
        [(key_sum[kv] * scale).astype(bf16) for kv in range(kv_per)], axis=1
    )
    grad_value[...] = jnp.concatenate(
        [value_sum[kv].astype(bf16) for kv in range(kv_per)], axis=1
    )


def attend_specs(seq_len, head_dim, group, kv_per):
    wide = pl.BlockSpec((seq_len, kv_per * group * head_dim), lambda s, h: (s, h))
    narrow = pl.BlockSpec((seq_len, kv_per * head_dim), lambda s, h: (s, h))
    seg_col = pl.BlockSpec((1, seq_len, 1), lambda s, h: (s, 0, 0))
    seg_row = pl.BlockSpec((1, 1, seq_len), lambda s, h: (s, 0, 0))
    return wide, narrow, seg_col, seg_row


def attend(query, key, value, segments, head_dim, group):
    seq_count, seq_len = segments.shape
    kv_count = key.shape[1] // head_dim
    kv_per = 2 if kv_count % 2 == 0 else kv_count
    steps = kv_count // kv_per
    wide, narrow, seg_col, seg_row = attend_specs(seq_len, head_dim, group, kv_per)
    logs = pl.BlockSpec((1, seq_len, kv_per * group), lambda s, h: (s * steps + h, 0, 0))
    heads = kv_count * group
    work = seq_count * heads * seq_len * seq_len

    def body(*refs):
        attend_kernel(head_dim, group, kv_per, *refs)

    return pl.pallas_call(
        body,
        grid=(seq_count, steps),
        in_specs=[wide, narrow, narrow, seg_col, seg_row],
        out_specs=[wide, logs],
        out_shape=[
            jax.ShapeDtypeStruct(query.shape, bf16),
            jax.ShapeDtypeStruct((seq_count * steps, seq_len, kv_per * group), f32),
        ],
        compiler_params=pltpu.CompilerParams(vmem_limit_bytes=40 * 1024 * 1024),
        cost_estimate=pl.CostEstimate(
            flops=4 * work * head_dim, bytes_accessed=8 * query.size, transcendentals=work
        ),
    )(query, key, value, segments[:, :, None], segments[:, None, :])


def attend_back(query, key, value, segments, mixed, grad_mixed, logs, head_dim, group):
    seq_count, seq_len = segments.shape
    kv_count = key.shape[1] // head_dim
    kv_per = logs.shape[2] // group
    steps = kv_count // kv_per
    wide, narrow, seg_col, seg_row = attend_specs(seq_len, head_dim, group, kv_per)
    log_spec = pl.BlockSpec((1, seq_len, kv_per * group), lambda s, h: (s * steps + h, 0, 0))
    heads = kv_count * group
    work = seq_count * heads * seq_len * seq_len

    def body(*refs):
        attend_back_kernel(head_dim, group, kv_per, *refs)

    return pl.pallas_call(
        body,
        grid=(seq_count, steps),
        in_specs=[wide, narrow, narrow, seg_col, seg_row, wide, wide, log_spec],
        out_specs=[wide, narrow, narrow],
        out_shape=[
            jax.ShapeDtypeStruct(query.shape, bf16),
            jax.ShapeDtypeStruct(key.shape, bf16),
            jax.ShapeDtypeStruct(key.shape, bf16),
        ],
        scratch_shapes=[
            pltpu.VMEM((kv_per, seq_len, head_dim), f32),
            pltpu.VMEM((kv_per, seq_len, head_dim), f32),
        ],
        compiler_params=pltpu.CompilerParams(vmem_limit_bytes=40 * 1024 * 1024),
        cost_estimate=pl.CostEstimate(
            flops=10 * work * head_dim, bytes_accessed=16 * query.size, transcendentals=work
        ),
    )(query, key, value, segments[:, :, None], segments[:, None, :], mixed, grad_mixed, logs)


def make_per_device():
    swap = [(0, 1), (1, 0)]

    def partner(values):
        return lax.ppermute(values, "ctx", swap)

    def in_order(side, own, other, axis):
        first = jnp.where(side == 0, own, other)
        second = jnp.where(side == 0, other, own)
        return jnp.concatenate([first, second], axis=axis)

    def pick(side, values, axis):
        return lax.dynamic_index_in_dim(values, side, axis, keepdims=False)

    def halves(side, weight, block):
        rows = weight.shape[0]
        cut = weight.reshape(rows, -1, 2, block)
        zero = cut[:, :, 0, :].reshape(rows, -1)
        one = cut[:, :, 1, :].reshape(rows, -1)
        return jnp.where(side == 0, zero, one), jnp.where(side == 0, one, zero)

    def gather_columns(side, weights, blocks):
        own, other = zip(*(halves(side, w, b) for w, b in zip(weights, blocks)))
        own = jnp.concatenate(own, axis=1)
        other = jnp.concatenate(other, axis=1)
        shard = in_order(side, own, partner(other), 0)
        return lax.all_gather(shard, "fsdp", axis=0, tiled=True)

    def scatter_rows(grad):
        return lax.psum_scatter(grad, "fsdp", scatter_dimension=0, tiled=True)

    def total_after(shard, earlier):
        shard, earlier = lax.optimization_barrier((shard, earlier))
        return lax.psum(shard, "replica"), earlier

    def restore_columns(side, shard, widths, blocks):
        cut = shard.reshape(2, -1, shard.shape[1])
        own = pick(side, cut, 0)
        other = partner(pick(1 - side, cut, 0))
        outs = []
        at = 0
        for width, block in zip(widths, blocks):
            mine = own[:, at : at + width].reshape(own.shape[0], -1, 1, block)
            theirs = other[:, at : at + width].reshape(own.shape[0], -1, 1, block)
            outs.append(in_order(side, mine, theirs, 2).reshape(own.shape[0], 2 * width).astype(f32))
            at += width
        return outs

    def gather_tokens(side, rows):
        return in_order(side, rows, partner(rows), 1)

    def own_sum(side, partial, seq_count, span_len):
        cut = partial.reshape(seq_count, 2, span_len, -1)
        own = pick(side, cut, 1)
        other = partner(pick(1 - side, cut, 1).astype(bf16))
        return (own + other.astype(f32)).reshape(seq_count * span_len, -1)

    def per_device(
        tokens,
        segments,
        attn_gain,
        query_weight,
        key_weight,
        value_weight,
        output_weight,
        query_gain,
        key_gain,
        ffn_gain,
        gate_weight,
        up_weight,
        down_weight,
        cotangent,
    ):
        side = lax.axis_index("ctx")
        shard_count = lax.axis_size("fsdp") * lax.axis_size("ctx")
        shard_at = lax.axis_index("fsdp") * lax.axis_size("ctx") + side
        seq_count, span_len, width = tokens.shape
        seq_len = segments.shape[1]
        own_count = seq_count * span_len
        tok_count = seq_count * seq_len
        gain_parts = (attn_gain, query_gain, key_gain, ffn_gain)
        gain_sizes = [g.shape[0] for g in gain_parts]
        packed = lax.all_gather(jnp.concatenate(gain_parts)[None], ("fsdp", "ctx"), axis=0, tiled=True)
        gains = []
        at = 0
        for size in gain_sizes:
            gains.append(packed[:, at : at + size].reshape(-1).astype(f32))
            at += size
        gain_one, gain_query, gain_key, gain_two = gains
        head_dim = gain_query.shape[0]
        head_count = query_weight.shape[1] // head_dim
        kv_count = key_weight.shape[1] // head_dim
        group = head_count // kv_count
        half_q = head_count * head_dim // 2
        half_k = kv_count * head_dim // 2
        feed_block = down_weight.shape[0]
        half_ff = gate_weight.shape[1] // 2
        attn_blocks = (group * head_dim, head_dim, head_dim)
        attn_widths = (half_q, half_k, half_k)

        weight_qkv = gather_columns(side, (query_weight, key_weight, value_weight), attn_blocks)
        out_rows = output_weight.shape[0]
        whole_heads = out_rows == group * head_dim
        if whole_heads:
            weight_out = lax.all_gather(output_weight, "fsdp", axis=0, tiled=True)
        else:
            full = lax.all_gather(output_weight, ("fsdp", "ctx"), axis=0, tiled=True)
            full = full.reshape(-1, 2, group * head_dim, width)
            weight_out = pick(side, full, 1).reshape(half_q, width)

        input_rows = tokens.astype(f32).reshape(own_count, width)
        factor_one = rms_scale(input_rows)
        normed_one = input_rows * factor_one
        hidden_own = (normed_one * gain_one).astype(bf16)
        hidden_in = gather_tokens(side, hidden_own.reshape(seq_count, span_len, width)).reshape(
            tok_count, width
        )
        cot_own = cotangent.reshape(own_count, width)
        cot_all = jnp.concatenate([cot_own, partner(cot_own)], axis=0)

        zeros_len = jnp.sum((segments == 0).astype(jnp.int32), axis=1, keepdims=True)
        ones_len = jnp.sum((segments == 1).astype(jnp.int32), axis=1, keepdims=True)
        starts = jnp.where(segments == 0, 0, jnp.where(segments == 1, zeros_len, zeros_len + ones_len))
        positions = (jnp.arange(seq_len, dtype=jnp.int32)[None, :] - starts).astype(f32)
        freq = jnp.power(f32(rope_base), -jnp.arange(head_dim // 2, dtype=f32) * 2.0 / head_dim)
        angle = positions.reshape(tok_count, 1) * freq
        cosine = jnp.cos(angle)
        sine = jnp.sin(angle)
        cos_two = jnp.concatenate([cosine, cosine], axis=-1)
        sin_two = jnp.concatenate([-sine, sine], axis=-1)

        def spread(table, count):
            return jnp.concatenate([table] * count, axis=1)

        def turn(values):
            half = head_dim // 2
            up = jnp.concatenate([values[:, half:], values[:, :half]], axis=1)
            down = jnp.concatenate([values[:, -half:], values[:, :-half]], axis=1)
            lane = jnp.arange(values.shape[1]) % head_dim
            return jnp.where(lane < half, up, down)

        def head_mean(values):
            count = values.shape[1] // head_dim
            ids = jnp.arange(values.shape[1]) // head_dim
            member = (ids[:, None] == jnp.arange(count)[None, :]).astype(f32)
            sums = jnp.dot(values, member, precision=lax.Precision.HIGHEST) / head_dim
            return jnp.dot(sums, member.T, precision=lax.Precision.HIGHEST)

        def head_norm(values):
            factor = lax.rsqrt(head_mean(values * values) + epsilon)
            return factor, values * factor

        qkv = dot_nn(hidden_in, weight_qkv)
        value_low = qkv[:, half_q + half_k :].astype(bf16)
        heads_pre = qkv[:, : half_q + half_k]
        both_count = (half_q + half_k) // head_dim
        gain_both = jnp.concatenate(
            [gain_query] * (half_q // head_dim) + [gain_key] * (half_k // head_dim)
        )
        cos_both = spread(cos_two, both_count)
        sin_both = spread(sin_two, both_count)
        factor_both, normed_both = head_norm(heads_pre)
        scaled_both = normed_both * gain_both
        rotated = (scaled_both * cos_both + turn(scaled_both) * sin_both).astype(bf16)
        query_low = rotated[:, :half_q]
        key_low = rotated[:, half_q:]
        mixed_low, logs = attend(query_low, key_low, value_low, segments, head_dim, group)

        branch = own_sum(side, dot_nn(mixed_low, weight_out), seq_count, span_len)
        resid = input_rows + branch
        factor_two = rms_scale(resid)
        normed_two = resid * factor_two
        second_own = (normed_two * gain_two).astype(bf16)
        second = jnp.concatenate([second_own, partner(second_own)], axis=0)

        weight_gu = gather_columns(side, (gate_weight, up_weight), (feed_block, feed_block))
        weight_down = lax.all_gather(down_weight, "fsdp", axis=0, tiled=True)
        gate_up = dot_nn(second, weight_gu).astype(bf16)
        gate = gate_up[:, :half_ff].astype(f32)
        up = gate_up[:, half_ff:].astype(f32)
        sigma = jax.nn.sigmoid(gate)
        silu = gate * sigma
        act = (silu * up).astype(bf16)
        feed = dot_nn(act, weight_down)
        feed_own = feed[:own_count] + partner(feed[own_count:].astype(bf16)).astype(f32)
        output = (resid + feed_own).astype(bf16).reshape(seq_count, span_len, width)

        grad_down = dot_tn(act, cot_all).astype(bf16)
        down_sum = lax.psum(scatter_rows(grad_down), "replica")
        grad_act = dot_nt(cot_all, weight_down)
        grad_gate = (grad_act * up * (sigma * (1.0 + gate * (1.0 - sigma)))).astype(bf16)
        grad_up = (grad_act * silu).astype(bf16)
        grad_gu = jnp.concatenate([grad_gate, grad_up], axis=1)
        two_part = dot_nt(grad_gu, weight_gu)
        grad_two = two_part[:own_count] + partner(two_part[own_count:].astype(bf16)).astype(f32)
        gu_shard, down_sum = total_after(
            scatter_rows(dot_tn(second, grad_gu).astype(bf16)), down_sum
        )
        grad_gain_two = jnp.sum(grad_two * normed_two, axis=0)
        grad_resid = cot_own.astype(f32) + norm_back(grad_two * gain_two, normed_two, factor_two)

        branch_own = grad_resid.astype(bf16).reshape(seq_count, span_len, width)
        grad_branch = gather_tokens(side, branch_own).reshape(tok_count, width)
        grad_mixed = dot_nt(grad_branch, weight_out).astype(bf16)
        grad_out = dot_tn(mixed_low, grad_branch)
        if whole_heads:
            out_shard = scatter_rows(grad_out.astype(bf16))
        else:
            blocks = grad_out.reshape(-1, 1, group * head_dim, width)
            full = in_order(side, blocks, jnp.zeros_like(blocks), 1).reshape(2 * half_q, width)
            full = lax.psum_scatter(full, ("fsdp", "ctx"), scatter_dimension=0, tiled=True)
            out_shard = full.astype(bf16)
        grad_query, grad_key, grad_value = attend_back(
            query_low, key_low, value_low, segments, mixed_low, grad_mixed, logs, head_dim, group
        )
        grad_both = jnp.concatenate([grad_query, grad_key], axis=1).astype(f32)
        grad_normed = grad_both * cos_both - turn(grad_both) * sin_both
        gain_sums = jnp.sum(grad_normed * normed_both, axis=0).reshape(both_count, head_dim)
        grad_gain_query = jnp.sum(gain_sums[: half_q // head_dim], axis=0)
        grad_gain_key = jnp.sum(gain_sums[half_q // head_dim :], axis=0)
        scaled_grad = grad_normed * gain_both
        pre_both = factor_both * (scaled_grad - normed_both * head_mean(scaled_grad * normed_both))
        grad_qkv = jnp.concatenate([pre_both.astype(bf16), grad_value], axis=1)
        qkv_part = scatter_rows(dot_tn(hidden_in, grad_qkv).astype(bf16))
        (qkv_shard, out_sum), gu_shard = total_after((qkv_part, out_shard), gu_shard)
        out_total = out_sum.astype(f32)
        down_total = down_sum.astype(f32)
        gate_total, up_total = restore_columns(
            side, gu_shard, (half_ff, half_ff), (feed_block, feed_block)
        )
        query_total, key_total, value_total = restore_columns(
            side, qkv_shard, attn_widths, attn_blocks
        )
        grad_one = own_sum(side, dot_nt(grad_qkv, weight_qkv), seq_count, span_len)
        grad_gain_one = jnp.sum(grad_one * normed_one, axis=0)
        input_grad = grad_resid + norm_back(grad_one * gain_one, normed_one, factor_one)

        gain_grads = (grad_gain_one, grad_gain_query, grad_gain_key, grad_gain_two)
        gain_pack = jnp.concatenate(
            [g.reshape(shard_count, -1) for g in gain_grads], axis=1
        )
        gain_pack = pick(shard_at, lax.psum(gain_pack, ("replica", "fsdp", "ctx")), 0)
        gain_totals = []
        at = 0
        for size in gain_sizes:
            gain_totals.append(gain_pack[at : at + size])
            at += size
        return (
            output,
            input_grad.reshape(seq_count, span_len, width),
            gain_totals[0],
            query_total,
            key_total,
            value_total,
            out_total,
            gain_totals[1],
            gain_totals[2],
            gain_totals[3],
            gate_total,
            up_total,
            down_total,
        )

    return per_device


def solution(mesh):
    in_specs = (
        P(("replica", "fsdp"), "ctx", None),
        P(("replica", "fsdp"), None),
        P(("fsdp", "ctx")),
        P(("fsdp", "ctx"), None),
        P(("fsdp", "ctx"), None),
        P(("fsdp", "ctx"), None),
        P(("fsdp", "ctx"), None),
        P(("fsdp", "ctx")),
        P(("fsdp", "ctx")),
        P(("fsdp", "ctx")),
        P(("fsdp", "ctx"), None),
        P(("fsdp", "ctx"), None),
        P(("fsdp", "ctx"), None),
        P(("replica", "fsdp"), "ctx", None),
    )
    out_specs = (
        P(("replica", "fsdp"), "ctx", None),
        P(("replica", "fsdp"), "ctx", None),
        P(("fsdp", "ctx")),
        P(("fsdp", "ctx"), None),
        P(("fsdp", "ctx"), None),
        P(("fsdp", "ctx"), None),
        P(("fsdp", "ctx"), None),
        P(("fsdp", "ctx")),
        P(("fsdp", "ctx")),
        P(("fsdp", "ctx")),
        P(("fsdp", "ctx"), None),
        P(("fsdp", "ctx"), None),
        P(("fsdp", "ctx"), None),
    )
    return jax.shard_map(
        make_per_device(), mesh=mesh, in_specs=in_specs, out_specs=out_specs, check_vma=False
    )
```
